32 devices in a mesh: anim: 8 (over y, x, core), mark: 4 (over z).
Axes of the slice: x: 2, y: 2, z: 4, core: 2. Of those that a mesh axis runs over, the one named last changes fastest.
Arguments:
- solution: float32 [2, 65536], P(None, 'anim'), may hold values from -6 to 6
- residual: float32 [2, 65536], P(None, 'anim'), may hold values from -18 to 18
- direction: float32 [2, 65536], P(None, 'anim'), may hold values from -18 to 18
- record_inverse: float32 [3, 65536], P(None, 'anim'), may hold values from -1 to 2, as said below
- precondition: float32 [3, 65536], P(None, 'anim'), may hold values from -0.3 to 0.6, as said below
- genetic_inverse: float32 [2, 2], replicated, may hold values from -1 to 1.6, as said below
- sire_slot: int32 [65536], P('anim'), may hold values from -1 to 12287, as said below
- dam_slot: int32 [65536], P('anim'), may hold values from -1 to 12287, as said below
- send_rows: int32 [8, 8, 512], P('anim'), may hold values from -1 to 8191, as said below
- genotyped_row: int32 [8192], P('anim'), may hold values from 0 to 8191, as said below
- genotypes: int32 [8192, 8192], P('anim', 'mark'), may hold values from 0 to 2
- allele_freq: float32 [8192], P('mark'), may hold values from 0.05 to 0.5
- marker_weight: float32 [8192], P('mark'), may hold values from 0.2 to 5
Outputs:
- new_solution: float32 [2, 65536], P(None, 'anim')
- new_residual: float32 [2, 65536], P(None, 'anim')
- new_direction: float32 [2, 65536], P(None, 'anim')
The draws below stay inside these ranges and needn't reach their ends.
Inputs may be any that keep to these rules, and one draw needn't show every extreme that they name: `sire_slot`: A slot below 0 marks an unknown parent, one from 0 to 8191 a row of the animal's own block, never the animal itself; a larger slot s names position (s - 8192) % 512 of the list that block (s - 8192) // 512 sends to the animal's block, and that position of send_rows is 0 or more. Every such used position is named by some animal of the receiving block. `dam_slot`: as for sire_slot. In each list send_rows[s, b, :] the used positions come first and hold distinct rows, the rest hold -1; a block's list to itself is empty; in every draw some block receives 512 used positions from every other block. `genotyped_row`: distinct within each block of 1024 genotype rows. `record_inverse`: each animal's triple (a, c, d) has a, d > 0 and |c| <= 0.5 sqrt(a d). `precondition`: each animal's triple (a, c, d) has a, d > 0 and |c| <= 0.5 sqrt(a d). `genetic_inverse`: Symmetric, diagonal entries positive, off-diagonal at most 0.6 times the root of their product in magnitude.
All inputs are finite; a program needn't handle non-finite values.
Results may differ from the reference program's by a relative error of at most 0.0001.
Values sent between devices are 32-bit elements; how exact they have to be, the bound alone decides.
A program may use at most 128 MiB of HBM per device.

```python
import math
import jax
import jax.numpy as jnp
from jax import lax

ANI_DEV = 8192
GEN_DEV = 1024
M = 8192
CAP = 512
SOURCES = 8
N = 65536
NG = 8192


def ramp_field(seed_key):
    position = jnp.arange(N, dtype=jnp.float32) / N
    base_draw = jnp.clip(jax.random.normal(seed_key, (2, N), jnp.float32), -6.0, 6.0)
    growth = 1.0 + 2.0 * position
    return (base_draw * growth[None, :]).astype(jnp.float32)


def draw_residual(key, part):
    return ramp_field(jax.random.fold_in(key, 11))


def draw_direction(key, part):
    return ramp_field(jax.random.fold_in(key, 12))


def sym_triple(seed_key, lower, upper):
    subkeys = jax.random.split(seed_key, 3)
    diag_one = jax.random.uniform(subkeys[0], (N,), jnp.float32, lower, upper)
    diag_two = jax.random.uniform(subkeys[1], (N,), jnp.float32, lower, upper)
    correlation = jax.random.uniform(subkeys[2], (N,), jnp.float32, -0.5, 0.5)
    return jnp.stack([diag_one, correlation * jnp.sqrt(diag_one * diag_two), diag_two]).astype(jnp.float32)


def draw_record_inverse(key, part):
    return sym_triple(jax.random.fold_in(key, 21), 0.2, 2.0)


def draw_precondition(key, part):
    return sym_triple(jax.random.fold_in(key, 22), 0.15, 0.6)


def draw_genetic_inverse(key, part):
    subkeys = jax.random.split(jax.random.fold_in(key, 31), 2)
    diagonal = jax.random.uniform(subkeys[0], (2,), jnp.float32, 0.8, 1.6)
    correlation = jax.random.uniform(subkeys[1], (), jnp.float32, -0.6, 0.6)
    off_diag = correlation * jnp.sqrt(diagonal[0] * diagonal[1])
    return jnp.stack([jnp.stack([diagonal[0], off_diag]), jnp.stack([off_diag, diagonal[1]])]).astype(jnp.float32)


def pedigree_plan(key):
    subkeys = jax.random.split(jax.random.fold_in(key, 101), 6)
    level_pick = jax.random.randint(subkeys[0], (SOURCES,), 0, 3)
    levels = jnp.array([CAP, CAP // 2, CAP // 4], dtype=jnp.int32)[level_pick]
    lowest = levels // 2
    spans = levels - lowest + 1
    counts = lowest[None, :] + jax.random.randint(subkeys[1], (SOURCES, SOURCES), 0, 1 << 20) % spans[None, :]
    full_block = jax.random.randint(subkeys[2], (), 0, SOURCES - 1)
    columns = jnp.arange(SOURCES, dtype=jnp.int32)
    counts = jnp.where(columns[None, :] == full_block, CAP, counts)
    counts = jnp.where(columns[:, None] == columns[None, :], 0, counts).astype(jnp.int32)
    offsets = jax.random.randint(subkeys[3], (SOURCES, SOURCES), 0, ANI_DEV)
    offsets = offsets.at[SOURCES - 1, full_block].set(ANI_DEV - 1)
    strides = 2 * jax.random.randint(subkeys[4], (SOURCES, SOURCES), 0, ANI_DEV // 2) + 1
    position = jnp.arange(CAP, dtype=jnp.int32)
    listed = (offsets[:, :, None] + position[None, None, :] * strides[:, :, None]) % ANI_DEV
    send_rows = jnp.where(position[None, None, :] < counts[:, :, None], listed, -1).astype(jnp.int32)
    slot_total = SOURCES * CAP
    reference_ids = jnp.arange(2 * ANI_DEV, dtype=jnp.int32)
    ghost_slot = reference_ids % slot_total
    source_block = ghost_slot // CAP
    ghost_pos = ghost_slot % CAP
    counts_in = counts.T[:, source_block]
    living = ghost_pos[None, :] < counts_in
    local_rows = jax.random.randint(subkeys[5], (SOURCES, 2 * ANI_DEV), 0, ANI_DEV)
    fallback = jnp.where((reference_ids % 2 == 0)[None, :], -1, local_rows)
    choices_made = jnp.where(living, ANI_DEV + ghost_slot[None, :], fallback)
    perm_keys = jax.random.split(jax.random.fold_in(key, 202), SOURCES)
    orders = jax.vmap(lambda block_key: jax.random.permutation(block_key, 2 * ANI_DEV))(perm_keys)
    shuffled = jnp.take_along_axis(choices_made, orders, axis=1)
    own_rows = jnp.arange(ANI_DEV, dtype=jnp.int32)[None, :]
    sire_part = shuffled[:, :ANI_DEV]
    dam_part = shuffled[:, ANI_DEV:]
    sire_part = jnp.where(sire_part == own_rows, (sire_part + 1) % ANI_DEV, sire_part)
    dam_part = jnp.where(dam_part == own_rows, (dam_part + 1) % ANI_DEV, dam_part)
    return (send_rows, sire_part.reshape(N).astype(jnp.int32), dam_part.reshape(N).astype(jnp.int32))


def draw_send_rows(key, part):
    return pedigree_plan(key)[0]


def draw_sire_slot(key, part):
    return pedigree_plan(key)[1]


def draw_dam_slot(key, part):
    return pedigree_plan(key)[2]


def draw_genotyped_row(key, part):
    subkeys = jax.random.split(jax.random.fold_in(key, 303), SOURCES)

    def one_block(block_key):
        first_key, second_key = jax.random.split(block_key)
        middle = (1 + jax.random.permutation(first_key, ANI_DEV - 2)).astype(jnp.int32)
        chosen = jnp.concatenate([jnp.array([0, ANI_DEV - 1], jnp.int32), middle[:GEN_DEV - 2]])
        return jax.random.permutation(second_key, chosen)
    return jax.vmap(one_block)(subkeys).reshape(NG).astype(jnp.int32)


def set_ends(result, key, least, high):
    longest = result.shape.index(max(result.shape))
    spots = []
    for shift in (0, 1):
        where = [jax.random.randint(jax.random.fold_in(key, axis), (), 0, length) for axis, length in enumerate(result.shape)]
        where[longest] = (where[longest] + shift) % result.shape[longest]
        spots.append(tuple(where))
    return result.at[spots[0]].set(least).at[spots[1]].set(high)


def shard_levels(rng, extent, shards, smallest, top_value):
    loudness = 1.0
    for dim, shards_of in shards:
        steps = jax.random.uniform(jax.random.fold_in(jax.random.fold_in(rng, 6), dim), (shards_of,), jnp.float32, smallest / len(shards), top_value / len(shards))
        loudness = loudness * jnp.repeat(jnp.exp(steps), extent[dim] // shards_of).reshape((-1,) + (1,) * (len(extent) - 1 - dim))
    return loudness


def scatter_about(stream_key, shape, deviation, limit, cuts=(), kind=jnp.bfloat16):
    loudness = shard_levels(stream_key, shape, cuts, -0.22, 0.18) if cuts else 1.0
    values = jax.random.normal(stream_key, shape, jnp.float32) * deviation * loudness
    return jnp.minimum(jnp.maximum(values, -limit), limit).astype(kind)


def setup_inputs(seed: int = 0) -> dict:
    seeds = jax.random.split(jax.random.key(seed), 14)
    return {
        "solution": scatter_about(seeds[0], (2, N), 1.0, 6.0, ((1, 8),), jnp.float32),
        "residual": draw_residual(jax.random.fold_in(seeds[13], 71), 0),
        "direction": draw_direction(jax.random.fold_in(seeds[13], 71), 0),
        "record_inverse": draw_record_inverse(jax.random.fold_in(seeds[13], 71), 0),
        "precondition": draw_precondition(jax.random.fold_in(seeds[13], 71), 0),
        "genetic_inverse": draw_genetic_inverse(jax.random.fold_in(seeds[13], 71), 0),
        "sire_slot": draw_sire_slot(jax.random.fold_in(seeds[13], 71), 0),
        "dam_slot": draw_dam_slot(jax.random.fold_in(seeds[13], 71), 0),
        "send_rows": draw_send_rows(jax.random.fold_in(seeds[13], 71), 0),
        "genotyped_row": draw_genotyped_row(jax.random.fold_in(seeds[13], 71), 0),
        "genotypes": set_ends(jax.random.randint(seeds[10], (NG, M), 0, 3), jax.random.fold_in(seeds[10], 1), 0, 2).astype(jnp.int32),
        "allele_freq": jnp.clip(0.05 + 0.45 * jax.random.uniform(seeds[11], (M,), jnp.float32) ** shard_levels(seeds[11], (M,), ((0, 4),), -0.2, 0.2), 0.05, 0.5),
        "marker_weight": jnp.clip(jnp.exp(math.log(5.0) - 3.218876 * jax.random.uniform(seeds[12], (M,), jnp.float32) ** shard_levels(seeds[12], (M,), ((0, 4),), -0.2, 0.2)), 0.2, 5.0),
    }


def apply_block(triple, vector):
    upper_row = triple[0] * vector[0] + triple[1] * vector[1]
    lower_row = triple[1] * vector[0] + triple[2] * vector[1]
    return jnp.stack([upper_row, lower_row])


def genetic_apply(matrix, vector):
    upper_row = matrix[0, 0] * vector[0] + matrix[0, 1] * vector[1]
    lower_row = matrix[1, 0] * vector[0] + matrix[1, 1] * vector[1]
    return jnp.stack([upper_row, lower_row])


def global_parent(slot, block_ids, send_rows):
    ghost_slot = slot - ANI_DEV
    source_block = jnp.clip(ghost_slot // CAP, 0, SOURCES - 1).astype(jnp.int32)
    position = jnp.clip(ghost_slot % CAP, 0, CAP - 1).astype(jnp.int32)
    remote_row = send_rows[source_block, block_ids, position]
    remote_index = source_block * ANI_DEV + remote_row
    local_index = block_ids * ANI_DEV + slot
    chosen = jnp.where(slot < 0, N, jnp.where(slot < ANI_DEV, local_index, remote_index))
    return chosen.astype(jnp.int32)


def pedigree_apply(direction, sire_slot, dam_slot, send_rows):
    block_ids = (jnp.arange(N, dtype=jnp.int32) // ANI_DEV).astype(jnp.int32)
    sire_index = global_parent(sire_slot, block_ids, send_rows)
    dam_index = global_parent(dam_slot, block_ids, send_rows)
    padded = jnp.concatenate([direction, jnp.zeros((2, 1), jnp.float32)], axis=1)
    known_count = (sire_slot >= 0).astype(jnp.float32) + (dam_slot >= 0).astype(jnp.float32)
    factor = 1.0 / (1.0 - 0.25 * known_count)
    sampling = factor * (direction - 0.5 * (padded[:, sire_index] + padded[:, dam_index]))
    spread = jnp.zeros((2, N + 1), jnp.float32)
    spread = spread.at[:, sire_index].add(-0.5 * sampling)
    spread = spread.at[:, dam_index].add(-0.5 * sampling)
    return sampling + spread[:, :N]


def genomic_apply(direction, genotyped_row, genotypes, allele_freq, marker_weight):
    owner_block = (jnp.arange(NG, dtype=jnp.int32) // GEN_DEV).astype(jnp.int32)
    animal_index = (owner_block * ANI_DEV + genotyped_row).astype(jnp.int32)
    picked = direction[:, animal_index]
    code_blocks = genotypes.reshape(SOURCES, GEN_DEV, M)
    picked_blocks = picked.reshape(2, SOURCES, GEN_DEV).transpose(1, 0, 2)

    def accumulate(running, pair):
        codes_block, picked_block = pair
        centered = codes_block.astype(jnp.float32) - 2.0 * allele_freq[None, :]
        return running + jnp.dot(picked_block, centered, precision=lax.Precision.HIGHEST), None

    marker_total, _ = lax.scan(accumulate, jnp.zeros((2, M), jnp.float32), (code_blocks, picked_blocks))
    scaled = marker_total * marker_weight[None, :] / M

    def project(codes_block):
        centered = codes_block.astype(jnp.float32) - 2.0 * allele_freq[None, :]
        return lax.dot_general(scaled, centered, (((1,), (1,)), ((), ())), precision=lax.Precision.HIGHEST)

    projected = lax.map(project, code_blocks)
    genomic = projected.transpose(1, 0, 2).reshape(2, NG)
    return jnp.zeros((2, N), jnp.float32).at[:, animal_index].add(genomic)


def reference(solution, residual, direction, record_inverse, precondition, genetic_inverse, sire_slot, dam_slot, send_rows, genotyped_row, genotypes, allele_freq, marker_weight):
    pedigree_term = pedigree_apply(direction, sire_slot, dam_slot, send_rows)
    genomic_term = genomic_apply(direction, genotyped_row, genotypes, allele_freq, marker_weight)
    image = apply_block(record_inverse, direction) + genetic_apply(genetic_inverse, pedigree_term + genomic_term)
    scaled_residual = apply_block(precondition, residual)
    old_product = jnp.sum(residual * scaled_residual)
    step_size = old_product / jnp.sum(direction * image)
    new_solution = solution + step_size * direction
    new_residual = residual - step_size * image
    new_scaled = apply_block(precondition, new_residual)
    new_product = jnp.sum(new_residual * new_scaled)
    new_direction = new_scaled + (new_product / old_product) * direction
    return (new_solution, new_residual, new_direction)
```

```python
import functools

import jax
import jax.numpy as jnp
from jax import lax
from jax.experimental import pallas as pl
from jax.experimental.pallas import tpu as pltpu
from jax.sharding import PartitionSpec as P

LANES = 128
WIDE = 256
STEP = 512
MESH = pl.DeviceIdType.MESH


def take(row, lane, like):
    table = jnp.broadcast_to(row, like.shape)
    return jnp.take_along_axis(table, lane, axis=1, mode="promise_in_bounds")


def split2(value):
    upper = value.astype(jnp.bfloat16).astype(jnp.float32)
    return upper, value - upper


def split3(value):
    upper, rest = split2(value)
    middle, lower = split2(rest)
    return upper, middle, lower


def scatter_product(index, values, height):
    high = index >> 8
    low = index & (WIDE - 1)
    count = index.shape[1]
    rows = lax.broadcasted_iota(jnp.int32, (height, count), 0) == high
    lanes = lax.broadcasted_iota(jnp.int32, (WIDE, count), 0) == low
    parts = []
    for value in values:
        for part in split2(value):
            parts.append(jnp.where(rows, part, 0.0).astype(jnp.bfloat16))
    left = jnp.concatenate(parts, axis=0)
    right = jnp.where(lanes, 1.0, 0.0).astype(jnp.bfloat16)
    return lax.dot_general(
        left, right, (((1,), (1,)), ((), ())), preferred_element_type=jnp.float32
    )


def kernel(
    blocks,
    layers,
    direction,
    residual,
    record_inverse,
    precondition,
    genetic,
    sire,
    dam,
    sire_flat,
    dam_flat,
    send_rows,
    picked_row,
    picked_flat,
    freq,
    weight,
    genotypes,
    image_out,
    coef_out,
    codes,
    codes_half,
    table,
    outgoing,
    ghosts,
    outbound,
    inbound,
    sampling,
    spread,
    gathered,
    marker_parts,
    row_parts,
    dots,
    code_sem,
    ghost_send,
    ghost_recv,
    back_send,
    back_recv,
    marker_send,
    marker_recv,
    row_send,
    row_recv,
    dot_send,
    dot_recv,
):
    animals = direction.shape[1]
    rows = animals // LANES
    capacity = send_rows.shape[1]
    spots = capacity // LANES
    gen_rows = picked_row.shape[0]
    markers = freq.shape[1]
    local_high = animals // WIDE
    full_high = local_high + blocks * capacity // WIDE
    chunks = codes.shape[0]
    chunk_rows = codes.shape[1]
    me = lax.axis_index("anim")
    layer = lax.axis_index("mark")

    def fetch(c):
        return pltpu.make_async_copy(
            genotypes.at[pl.ds(c * chunk_rows, chunk_rows)], codes.at[c], code_sem.at[c]
        )

    for c in range(chunks):
        fetch(c).start()

    barrier = pltpu.get_barrier_semaphore()
    for off in range(1, blocks):
        pl.semaphore_signal(
            barrier, inc=1, device_id={"anim": lax.rem(me + off, blocks)}, device_id_type=MESH
        )
    for off in range(1, layers):
        pl.semaphore_signal(
            barrier, inc=1, device_id={"mark": lax.rem(layer + off, layers)}, device_id_type=MESH
        )

    def spread_out(axis, size, mine, buffer_from, buffer_to, send_sem, recv_sem, by_target):
        copies = []
        for off in range(1, size):
            peer = lax.rem(mine + off, size)
            copy = pltpu.make_async_remote_copy(
                src_ref=buffer_from.at[peer] if by_target else buffer_from.at[mine],
                dst_ref=buffer_to.at[mine],
                send_sem=send_sem.at[off - 1],
                recv_sem=recv_sem.at[mine],
                device_id={axis: peer},
                device_id_type=MESH,
            )
            copy.start()
            copies.append(copy)
        return copies

    def arrive(axis, size, mine, buffer, send_sem, recv_sem):
        for off in range(1, size):
            peer = lax.rem(mine + off, size)
            pltpu.make_async_remote_copy(
                src_ref=buffer.at[peer],
                dst_ref=buffer.at[peer],
                send_sem=send_sem.at[off - 1],
                recv_sem=recv_sem.at[peer],
                device_id={axis: peer},
                device_id_type=MESH,
            ).wait_recv()

    for r in range(rows):
        pair = direction[:, r * LANES : (r + 1) * LANES]
        table[0, r : r + 1, :] = pair[0:1]
        table[1, r : r + 1, :] = pair[1:2]

    wanted = [send_rows[:, k * LANES : (k + 1) * LANES] for k in range(spots)]
    wanted.append(picked_row[...])
    wanted_high = [index >> 7 for index in wanted]
    wanted_lane = [index & (LANES - 1) for index in wanted]

    def pick_wanted(r, found):
        out = []
        for high, lane, (first, second) in zip(wanted_high, wanted_lane, found):
            here = high == r
            out.append(
                (
                    jnp.where(here, take(table[0, pl.ds(r, 1), :], lane, lane), first),
                    jnp.where(here, take(table[1, pl.ds(r, 1), :], lane, lane), second),
                )
            )
        return tuple(out)

    zeros = tuple((jnp.zeros(i.shape, jnp.float32),) * 2 for i in wanted)
    found = lax.fori_loop(0, rows, pick_wanted, zeros, unroll=4)
    for k in range(spots):
        for trait in range(2):
            for b in range(blocks):
                outgoing[b, trait * spots + k : trait * spots + k + 1, :] = found[k][trait][b : b + 1]
    picked = found[spots]

    pl.semaphore_wait(barrier, blocks - 1 + layers - 1)
    ghost_copies = spread_out("anim", blocks, me, outgoing, ghosts, ghost_send, ghost_recv, True)
    ghosts[me] = jnp.zeros(ghosts.shape[1:], jnp.float32)

    picked_parts = [split3(value) for value in picked]
    total = jnp.zeros((6, markers), jnp.float32)
    per_chunk = chunk_rows // LANES
    for c in range(chunks):
        fetch(c).wait()
        codes_half[pl.ds(c * chunk_rows, chunk_rows), :] = (
            codes[c].astype(jnp.float32).astype(jnp.bfloat16)
        )
        lines = []
        for part in range(3):
            for trait in range(2):
                block = picked_parts[trait][part]
                lines.append(
                    jnp.concatenate(
                        [block[c * per_chunk + i : c * per_chunk + i + 1] for i in range(per_chunk)],
                        axis=1,
                    )
                )
        left = jnp.concatenate(lines, axis=0).astype(jnp.bfloat16)
        total = total + jnp.dot(
            left,
            codes_half[pl.ds(c * chunk_rows, chunk_rows), :],
            preferred_element_type=jnp.float32,
        )
    frequency = 2.0 * freq[...]
    sums = [jnp.sum(picked[trait]) for trait in range(2)]
    marker_parts[me] = jnp.concatenate(
        [
            (total[t : t + 1] + total[2 + t : 3 + t] + total[4 + t : 5 + t]) - sums[t] * frequency
            for t in range(2)
        ],
        axis=0,
    )
    marker_copies = spread_out(
        "anim", blocks, me, marker_parts, marker_parts, marker_send, marker_recv, False
    )

    slots = [sire[...], dam[...]]
    sums_of_parents = [jnp.zeros((rows, LANES), jnp.float32)] * 2
    known = (slots[0] >= 0).astype(jnp.float32) + (slots[1] >= 0).astype(jnp.float32)
    parents = []
    for slot in slots:
        high = slot >> 7
        lane = slot & (LANES - 1)

        def local(r, carry, high=high, lane=lane):
            here = high == r
            return tuple(
                jnp.where(here, take(table[t, pl.ds(r, 1), :], lane, lane), carry[t])
                for t in range(2)
            )

        zero = jnp.zeros((rows, LANES), jnp.float32)
        parents.append(lax.fori_loop(0, rows, local, (zero, zero), unroll=2))
    arrive("anim", blocks, me, ghosts, ghost_send, ghost_recv)
    for which, slot in enumerate(slots):
        high = slot >> 7
        lane = slot & (LANES - 1)

        def remote(source, carry, high=high, lane=lane):
            for k in range(spots):
                here = high == rows + source * spots + k
                carry = tuple(
                    jnp.where(
                        here,
                        take(ghosts[source, t * spots + k : t * spots + k + 1, :], lane, lane),
                        carry[t],
                    )
                    for t in range(2)
                )
            return carry

        parents[which] = lax.fori_loop(0, blocks, remote, parents[which])
    factor = 1.0 / (1.0 - 0.25 * known)
    for t in range(2):
        sampling[t] = factor * (table[t] - 0.5 * (parents[0][t] + parents[1][t]))

    spread[...] = jnp.zeros(spread.shape, jnp.float32)
    lines_per_step = STEP // LANES

    def sampling_lines(t, j):
        return jnp.concatenate(
            [sampling[t, pl.ds(j * lines_per_step + i, 1), :] for i in range(lines_per_step)], axis=1
        )

    def offspring(j, carry):
        values = [-0.5 * sampling_lines(t, j) for t in range(2)]
        at = pl.ds(pl.multiple_of(j * STEP, STEP), STEP)
        spread[...] += scatter_product(sire_flat[:, at], values, full_high) + scatter_product(
            dam_flat[:, at], values, full_high
        )
        return carry

    lax.fori_loop(0, animals // STEP, offspring, 0)
    per_source = capacity // WIDE
    for t in range(2):
        both = spread[2 * t * full_high : (2 * t + 1) * full_high] + spread[
            (2 * t + 1) * full_high : (2 * t + 2) * full_high
        ]
        gathered[t] = both[:local_high]
        for b in range(blocks):
            for i in range(per_source):
                h = local_high + b * per_source + i
                for half in range(2):
                    at = t * spots + 2 * i + half
                    outbound[b, at : at + 1, :] = both[h : h + 1, half * LANES : (half + 1) * LANES]
    back_copies = spread_out("anim", blocks, me, outbound, inbound, back_send, back_recv, True)
    inbound[me] = jnp.zeros(inbound.shape[1:], jnp.float32)

    arrive("anim", blocks, me, marker_parts, marker_send, marker_recv)
    marker_total = marker_parts[0]
    for b in range(1, blocks):
        marker_total = marker_total + marker_parts[b]
    scaled = marker_total * weight[...] / (markers * layers)
    offset = jnp.sum(scaled * frequency, axis=1, keepdims=True)
    left = jnp.concatenate(split3(scaled), axis=0).astype(jnp.bfloat16)
    row_sums = lax.dot_general(
        left, codes_half[...], (((1,), (1,)), ((), ())), preferred_element_type=jnp.float32
    )
    row_parts[layer] = row_sums[0:2] + row_sums[2:4] + row_sums[4:6] - offset
    row_copies = spread_out("mark", layers, layer, row_parts, row_parts, row_send, row_recv, False)

    arrive("anim", blocks, me, inbound, back_send, back_recv)

    def returned(b, carry):
        values = [
            jnp.concatenate(
                [inbound[b, t * spots + k : t * spots + k + 1, :] for k in range(spots)], axis=1
            )
            for t in range(2)
        ]
        return carry + scatter_product(send_rows[pl.ds(b, 1), :], values, local_high)

    added = lax.fori_loop(0, blocks, returned, jnp.zeros((4 * local_high, WIDE), jnp.float32))
    arrive("mark", layers, layer, row_parts, row_send, row_recv)
    genomic = row_parts[0]
    for z in range(1, layers):
        genomic = genomic + row_parts[z]
    added = added + scatter_product(picked_flat[...], [genomic[0:1], genomic[1:2]], local_high)
    for t in range(2):
        gathered[t] = (
            gathered[t]
            + added[2 * t * local_high : (2 * t + 1) * local_high]
            + added[(2 * t + 1) * local_high : (2 * t + 2) * local_high]
        )

    g00, g01, g10, g11 = genetic[0, 0], genetic[0, 1], genetic[1, 0], genetic[1, 1]

    def finish(j, carry):
        at = pl.ds(pl.multiple_of(j * STEP, STEP), STEP)
        d = direction[:, at]
        r = residual[:, at]
        rec = record_inverse[:, at]
        pre = precondition[:, at]
        d0, d1, r0, r1 = d[0:1], d[1:2], r[0:1], r[1:2]
        terms = [
            sampling_lines(t, j)
            + jnp.concatenate(
                [gathered[t, pl.ds(j * (STEP // WIDE) + i, 1), :] for i in range(STEP // WIDE)],
                axis=1,
            )
            for t in range(2)
        ]
        i0 = rec[0:1] * d0 + rec[1:2] * d1 + (g00 * terms[0] + g01 * terms[1])
        i1 = rec[1:2] * d0 + rec[2:3] * d1 + (g10 * terms[0] + g11 * terms[1])
        image_out[0:1, at] = i0
        image_out[1:2, at] = i1
        s0 = pre[0:1] * r0 + pre[1:2] * r1
        s1 = pre[1:2] * r0 + pre[2:3] * r1
        m0 = pre[0:1] * i0 + pre[1:2] * i1
        m1 = pre[1:2] * i0 + pre[2:3] * i1
        old, curve, cross, image = carry
        return (
            old + (r0 * s0 + r1 * s1),
            curve + (d0 * i0 + d1 * i1),
            cross + (i0 * s0 + i1 * s1),
            image + (i0 * m0 + i1 * m1),
        )

    zero = jnp.zeros((1, STEP), jnp.float32)
    products = lax.fori_loop(0, animals // STEP, finish, (zero,) * 4)
    lines = [
        sum(value[:, i * LANES : (i + 1) * LANES] for i in range(STEP // LANES))
        for value in products
    ]
    lines.append(jnp.zeros((4, LANES), jnp.float32))
    dots[me] = jnp.concatenate(lines, axis=0)
    dot_copies = spread_out("anim", blocks, me, dots, dots, dot_send, dot_recv, False)
    arrive("anim", blocks, me, dots, dot_send, dot_recv)
    whole = dots[0]
    for b in range(1, blocks):
        whole = whole + dots[b]
    sums = jnp.sum(whole, axis=1, keepdims=True)
    old, curve, cross, image = (sums[i : i + 1] for i in range(4))
    step = old / curve
    new = old - 2.0 * step * cross + step * step * image
    coef_out[...] = jnp.broadcast_to(jnp.concatenate([step, new / old], axis=0), coef_out.shape)
    for copy in ghost_copies + marker_copies + back_copies + row_copies + dot_copies:
        copy.wait_send()


def on_device(
    blocks,
    layers,
    solution,
    residual,
    direction,
    record_inverse,
    precondition,
    genetic_inverse,
    sire_slot,
    dam_slot,
    send_rows,
    genotyped_row,
    genotypes,
    allele_freq,
    marker_weight,
):
    animals = direction.shape[1]
    rows = animals // LANES
    capacity = send_rows.shape[2]
    gen, markers = genotypes.shape
    chunk_rows = 256
    lists = (blocks, 2 * capacity // LANES, LANES)
    full_high = (animals + blocks * capacity) // WIDE
    vmem = pl.BlockSpec(memory_space=pltpu.VMEM)
    dma = pltpu.SemaphoreType.DMA
    f32 = jnp.float32
    image, coef = pl.pallas_call(
        functools.partial(kernel, blocks, layers),
        out_shape=(
            jax.ShapeDtypeStruct((2, animals), f32),
            jax.ShapeDtypeStruct((2, LANES), f32),
        ),
        in_specs=[vmem] * 4
        + [pl.BlockSpec(memory_space=pltpu.SMEM)]
        + [vmem] * 9
        + [pl.BlockSpec(memory_space=pl.ANY)],
        out_specs=(vmem, vmem),
        scratch_shapes=[
            pltpu.VMEM((gen // chunk_rows, chunk_rows, markers), jnp.int32),
            pltpu.VMEM((gen, markers), jnp.bfloat16),
            pltpu.VMEM((2, rows, LANES), f32),
            pltpu.VMEM(lists, f32),
            pltpu.VMEM(lists, f32),
            pltpu.VMEM(lists, f32),
            pltpu.VMEM(lists, f32),
            pltpu.VMEM((2, rows, LANES), f32),
            pltpu.VMEM((4 * full_high, WIDE), f32),
            pltpu.VMEM((2, animals // WIDE, WIDE), f32),
            pltpu.VMEM((blocks, 2, markers), f32),
            pltpu.VMEM((layers, 2, gen), f32),
            pltpu.VMEM((blocks, 8, LANES), f32),
            dma((gen // chunk_rows,)),
            dma((blocks - 1,)),
            dma((blocks,)),
            dma((blocks - 1,)),
            dma((blocks,)),
            dma((blocks - 1,)),
            dma((blocks,)),
            dma((layers - 1,)),
            dma((layers,)),
            dma((blocks - 1,)),
            dma((blocks,)),
        ],
        compiler_params=pltpu.CompilerParams(
            collective_id=0, has_side_effects=True, vmem_limit_bytes=50 * 2**20
        ),
    )(
        direction,
        residual,
        record_inverse,
        precondition,
        genetic_inverse,
        sire_slot.reshape(rows, LANES),
        dam_slot.reshape(rows, LANES),
        sire_slot.reshape(1, animals),
        dam_slot.reshape(1, animals),
        send_rows.reshape(blocks, capacity),
        genotyped_row.reshape(gen // LANES, LANES),
        genotyped_row.reshape(1, gen),
        allele_freq.reshape(1, markers),
        marker_weight.reshape(1, markers),
        genotypes,
    )
    step = coef[0, 0]
    ratio = coef[1, 0]
    new_residual = residual - step * image
    upper = precondition[0] * new_residual[0] + precondition[1] * new_residual[1]
    lower = precondition[1] * new_residual[0] + precondition[2] * new_residual[1]
    return (
        solution + step * direction,
        new_residual,
        jnp.stack([upper, lower]) + ratio * direction,
    )


def solution(mesh):
    return jax.shard_map(
        functools.partial(on_device, mesh.shape["anim"], mesh.shape["mark"]),
        mesh=mesh,
        in_specs=(
            P(None, "anim"),
            P(None, "anim"),
            P(None, "anim"),
            P(None, "anim"),
            P(None, "anim"),
            P(),
            P("anim"),
            P("anim"),
            P("anim", None, None),
            P("anim"),
            P("anim", "mark"),
            P("mark"),
            P("mark"),
        ),
        out_specs=(P(None, "anim"), P(None, "anim"), P(None, "anim")),
        check_vma=False,
    )
```

```python
import functools

import jax
import jax.numpy as jnp
from jax import lax
from jax.experimental import pallas as pl
from jax.experimental.pallas import tpu as pltpu
from jax.sharding import PartitionSpec as P

LANES = 128
WIDE = 256
STEP = 512
MESH = pl.DeviceIdType.MESH


def take(row, lane, like):
    table = jnp.broadcast_to(row, like.shape)
    return jnp.take_along_axis(table, lane, axis=1, mode="promise_in_bounds")


def split2(value):
    upper = value.astype(jnp.bfloat16).astype(jnp.float32)
    return upper, value - upper


def split3(value):
    upper, rest = split2(value)
    middle, lower = split2(rest)
    return upper, middle, lower


def scatter_product(index, values, height):
    high = index >> 8
    low = index & (WIDE - 1)
    count = index.shape[1]
    rows = lax.broadcasted_iota(jnp.int32, (height, count), 0) == high
    lanes = lax.broadcasted_iota(jnp.int32, (WIDE, count), 0) == low
    parts = []
    for value in values:
        for part in split2(value):
            parts.append(jnp.where(rows, part, 0.0).astype(jnp.bfloat16))
    left = jnp.concatenate(parts, axis=0)
    right = jnp.where(lanes, 1.0, 0.0).astype(jnp.bfloat16)
    return lax.dot_general(
        left, right, (((1,), (1,)), ((), ())), preferred_element_type=jnp.float32
    )


def kernel(
    blocks,
    layers,
    direction_hbm,
    residual_hbm,
    record_inverse_hbm,
    precondition_hbm,
    genetic_hbm,
    sire_hbm,
    dam_hbm,
    sire_flat_hbm,
    dam_flat_hbm,
    send_rows_hbm,
    picked_row_hbm,
    picked_flat_hbm,
    freq_hbm,
    weight_hbm,
    genotypes,
    solution_hbm,
    image_out,
    coef_out,
    direction,
    residual,
    precondition,
    solution,
    record_inverse,
    genetic,
    sire,
    dam,
    sire_flat,
    dam_flat,
    send_rows,
    picked_row,
    picked_flat,
    freq,
    weight,
    input_sem,
    codes,
    codes_half,
    table,
    outgoing,
    ghosts,
    outbound,
    inbound,
    sampling,
    spread,
    gathered,
    marker_parts,
    row_parts,
    dots,
    code_sem,
    ghost_send,
    ghost_recv,
    back_send,
    back_recv,
    marker_send,
    marker_recv,
    row_send,
    row_recv,
    dot_send,
    dot_recv,
):
    animals = direction.shape[1]
    rows = animals // LANES
    capacity = send_rows.shape[1]
    spots = capacity // LANES
    gen_rows = picked_row.shape[0]
    markers = freq.shape[1]
    local_high = animals // WIDE
    full_high = local_high + blocks * capacity // WIDE
    chunks = codes.shape[0]
    chunk_rows = codes.shape[1]
    me = lax.axis_index("anim")
    layer = lax.axis_index("mark")

    def fetch(c):
        return pltpu.make_async_copy(
            genotypes.at[pl.ds(c * chunk_rows, chunk_rows)], codes.at[c], code_sem.at[c]
        )

    loads = [
        pltpu.make_async_copy(source, target, input_sem.at[i])
        for i, (source, target) in enumerate(
            [
                (direction_hbm, direction),
                (send_rows_hbm, send_rows),
                (picked_row_hbm, picked_row),
                (freq_hbm, freq),
                (sire_hbm, sire),
                (dam_hbm, dam),
                (sire_flat_hbm, sire_flat),
                (dam_flat_hbm, dam_flat),
                (weight_hbm, weight),
                (picked_flat_hbm, picked_flat),
                (genetic_hbm, genetic),
                (record_inverse_hbm, record_inverse),
                (residual_hbm, residual),
                (precondition_hbm, precondition),
                (solution_hbm, solution),
            ]
        )
    ]
    for load in loads[:4]:
        load.start()
    for c in range(chunks):
        fetch(c).start()
    for load in loads[4:]:
        load.start()

    barrier = pltpu.get_barrier_semaphore()
    for off in range(1, blocks):
        pl.semaphore_signal(
            barrier, inc=1, device_id={"anim": lax.rem(me + off, blocks)}, device_id_type=MESH
        )
    for off in range(1, layers):
        pl.semaphore_signal(
            barrier, inc=1, device_id={"mark": lax.rem(layer + off, layers)}, device_id_type=MESH
        )

    def spread_out(axis, size, mine, buffer_from, buffer_to, send_sem, recv_sem, by_target):
        copies = []
        for off in range(1, size):
            peer = lax.rem(mine + off, size)
            copy = pltpu.make_async_remote_copy(
                src_ref=buffer_from.at[peer] if by_target else buffer_from.at[mine],
                dst_ref=buffer_to.at[mine],
                send_sem=send_sem.at[off - 1],
                recv_sem=recv_sem.at[mine],
                device_id={axis: peer},
                device_id_type=MESH,
            )
            copy.start()
            copies.append(copy)
        return copies

    def arrive(axis, size, mine, buffer, send_sem, recv_sem):
        for off in range(1, size):
            peer = lax.rem(mine + off, size)
            pltpu.make_async_remote_copy(
                src_ref=buffer.at[peer],
                dst_ref=buffer.at[peer],
                send_sem=send_sem.at[off - 1],
                recv_sem=recv_sem.at[peer],
                device_id={axis: peer},
                device_id_type=MESH,
            ).wait_recv()

    for load in loads[:3]:
        load.wait()
    for r in range(rows):
        pair = direction[:, r * LANES : (r + 1) * LANES]
        table[0, r : r + 1, :] = pair[0:1]
        table[1, r : r + 1, :] = pair[1:2]

    wanted = [send_rows[:, k * LANES : (k + 1) * LANES] for k in range(spots)]
    wanted.append(picked_row[...])
    wanted_high = [index >> 7 for index in wanted]
    wanted_lane = [index & (LANES - 1) for index in wanted]

    def pick_wanted(r, found):
        out = []
        for high, lane, (first, second) in zip(wanted_high, wanted_lane, found):
            here = high == r
            out.append(
                (
                    jnp.where(here, take(table[0, pl.ds(r, 1), :], lane, lane), first),
                    jnp.where(here, take(table[1, pl.ds(r, 1), :], lane, lane), second),
                )
            )
        return tuple(out)

    zeros = tuple((jnp.zeros(i.shape, jnp.float32),) * 2 for i in wanted)
    found = lax.fori_loop(0, rows, pick_wanted, zeros, unroll=4)
    for k in range(spots):
        for trait in range(2):
            for b in range(blocks):
                outgoing[b, trait * spots + k : trait * spots + k + 1, :] = found[k][trait][b : b + 1]
    picked = found[spots]

    pl.semaphore_wait(barrier, blocks - 1 + layers - 1)
    ghost_copies = spread_out("anim", blocks, me, outgoing, ghosts, ghost_send, ghost_recv, True)
    ghosts[me] = jnp.zeros(ghosts.shape[1:], jnp.float32)

    picked_parts = [split3(value) for value in picked]
    total = jnp.zeros((6, markers), jnp.float32)
    per_chunk = chunk_rows // LANES
    for c in range(chunks):
        fetch(c).wait()
        codes_half[pl.ds(c * chunk_rows, chunk_rows), :] = (
            codes[c].astype(jnp.float32).astype(jnp.bfloat16)
        )
        lines = []
        for part in range(3):
            for trait in range(2):
                block = picked_parts[trait][part]
                lines.append(
                    jnp.concatenate(
                        [block[c * per_chunk + i : c * per_chunk + i + 1] for i in range(per_chunk)],
                        axis=1,
                    )
                )
        left = jnp.concatenate(lines, axis=0).astype(jnp.bfloat16)
        total = total + jnp.dot(
            left,
            codes_half[pl.ds(c * chunk_rows, chunk_rows), :],
            preferred_element_type=jnp.float32,
        )
    loads[3].wait()
    frequency = 2.0 * freq[...]
    sums = [jnp.sum(picked[trait]) for trait in range(2)]
    marker_parts[me] = jnp.concatenate(
        [
            (total[t : t + 1] + total[2 + t : 3 + t] + total[4 + t : 5 + t]) - sums[t] * frequency
            for t in range(2)
        ],
        axis=0,
    )
    marker_copies = spread_out(
        "anim", blocks, me, marker_parts, marker_parts, marker_send, marker_recv, False
    )

    for load in loads[4:8]:
        load.wait()
    slots = [sire[...], dam[...]]
    sums_of_parents = [jnp.zeros((rows, LANES), jnp.float32)] * 2
    known = (slots[0] >= 0).astype(jnp.float32) + (slots[1] >= 0).astype(jnp.float32)
    parents = []
    for slot in slots:
        high = slot >> 7
        lane = slot & (LANES - 1)

        def local(r, carry, high=high, lane=lane):
            here = high == r
            return tuple(
                jnp.where(here, take(table[t, pl.ds(r, 1), :], lane, lane), carry[t])
                for t in range(2)
            )

        zero = jnp.zeros((rows, LANES), jnp.float32)
        parents.append(lax.fori_loop(0, rows, local, (zero, zero), unroll=2))
    arrive("anim", blocks, me, ghosts, ghost_send, ghost_recv)
    for which, slot in enumerate(slots):
        high = slot >> 7
        lane = slot & (LANES - 1)

        def remote(source, carry, high=high, lane=lane):
            for k in range(spots):
                here = high == rows + source * spots + k
                carry = tuple(
                    jnp.where(
                        here,
                        take(ghosts[source, t * spots + k : t * spots + k + 1, :], lane, lane),
                        carry[t],
                    )
                    for t in range(2)
                )
            return carry

        parents[which] = lax.fori_loop(0, blocks, remote, parents[which])
    factor = 1.0 / (1.0 - 0.25 * known)
    for t in range(2):
        sampling[t] = factor * (table[t] - 0.5 * (parents[0][t] + parents[1][t]))

    spread[...] = jnp.zeros(spread.shape, jnp.float32)
    lines_per_step = STEP // LANES

    def sampling_lines(t, j):
        return jnp.concatenate(
            [sampling[t, pl.ds(j * lines_per_step + i, 1), :] for i in range(lines_per_step)], axis=1
        )

    def offspring(j, carry):
        values = [-0.5 * sampling_lines(t, j) for t in range(2)]
        at = pl.ds(pl.multiple_of(j * STEP, STEP), STEP)
        spread[...] += scatter_product(sire_flat[:, at], values, full_high) + scatter_product(
            dam_flat[:, at], values, full_high
        )
        return carry

    lax.fori_loop(0, animals // STEP, offspring, 0)
    per_source = capacity // WIDE
    for t in range(2):
        both = spread[2 * t * full_high : (2 * t + 1) * full_high] + spread[
            (2 * t + 1) * full_high : (2 * t + 2) * full_high
        ]
        gathered[t] = both[:local_high]
        for b in range(blocks):
            for i in range(per_source):
                h = local_high + b * per_source + i
                for half in range(2):
                    at = t * spots + 2 * i + half
                    outbound[b, at : at + 1, :] = both[h : h + 1, half * LANES : (half + 1) * LANES]
    back_copies = spread_out("anim", blocks, me, outbound, inbound, back_send, back_recv, True)
    inbound[me] = jnp.zeros(inbound.shape[1:], jnp.float32)

    arrive("anim", blocks, me, marker_parts, marker_send, marker_recv)
    loads[8].wait()
    marker_total = marker_parts[0]
    for b in range(1, blocks):
        marker_total = marker_total + marker_parts[b]
    scaled = marker_total * weight[...] / (markers * layers)
    offset = jnp.sum(scaled * frequency, axis=1, keepdims=True)
    left = jnp.concatenate(split3(scaled), axis=0).astype(jnp.bfloat16)
    row_sums = lax.dot_general(
        left, codes_half[...], (((1,), (1,)), ((), ())), preferred_element_type=jnp.float32
    )
    row_parts[layer] = row_sums[0:2] + row_sums[2:4] + row_sums[4:6] - offset
    row_copies = spread_out("mark", layers, layer, row_parts, row_parts, row_send, row_recv, False)

    arrive("anim", blocks, me, inbound, back_send, back_recv)

    def returned(b, carry):
        values = [
            jnp.concatenate(
                [inbound[b, t * spots + k : t * spots + k + 1, :] for k in range(spots)], axis=1
            )
            for t in range(2)
        ]
        return carry + scatter_product(send_rows[pl.ds(b, 1), :], values, local_high)

    added = lax.fori_loop(0, blocks, returned, jnp.zeros((4 * local_high, WIDE), jnp.float32))
    for load in loads[9:]:
        load.wait()
    arrive("mark", layers, layer, row_parts, row_send, row_recv)
    genomic = row_parts[0]
    for z in range(1, layers):
        genomic = genomic + row_parts[z]
    added = added + scatter_product(picked_flat[...], [genomic[0:1], genomic[1:2]], local_high)
    for t in range(2):
        gathered[t] = (
            gathered[t]
            + added[2 * t * local_high : (2 * t + 1) * local_high]
            + added[(2 * t + 1) * local_high : (2 * t + 2) * local_high]
        )

    g00, g01, g10, g11 = (genetic[a : a + 1, b : b + 1] for a in range(2) for b in range(2))

    def finish(j, carry):
        at = pl.ds(pl.multiple_of(j * STEP, STEP), STEP)
        d = direction[:, at]
        r = residual[:, at]
        rec = record_inverse[:, at]
        pre = precondition[:, at]
        d0, d1, r0, r1 = d[0:1], d[1:2], r[0:1], r[1:2]
        terms = [
            sampling_lines(t, j)
            + jnp.concatenate(
                [gathered[t, pl.ds(j * (STEP // WIDE) + i, 1), :] for i in range(STEP // WIDE)],
                axis=1,
            )
            for t in range(2)
        ]
        i0 = rec[0:1] * d0 + rec[1:2] * d1 + (g00 * terms[0] + g01 * terms[1])
        i1 = rec[1:2] * d0 + rec[2:3] * d1 + (g10 * terms[0] + g11 * terms[1])
        image_out[0:1, at] = i0
        image_out[1:2, at] = i1
        s0 = pre[0:1] * r0 + pre[1:2] * r1
        s1 = pre[1:2] * r0 + pre[2:3] * r1
        m0 = pre[0:1] * i0 + pre[1:2] * i1
        m1 = pre[1:2] * i0 + pre[2:3] * i1
        old, curve, cross, image = carry
        return (
            old + (r0 * s0 + r1 * s1),
            curve + (d0 * i0 + d1 * i1),
            cross + (i0 * s0 + i1 * s1),
            image + (i0 * m0 + i1 * m1),
        )

    zero = jnp.zeros((1, STEP), jnp.float32)
    products = lax.fori_loop(0, animals // STEP, finish, (zero,) * 4)
    lines = [
        sum(value[:, i * LANES : (i + 1) * LANES] for i in range(STEP // LANES))
        for value in products
    ]
    lines.append(jnp.zeros((4, LANES), jnp.float32))
    dots[me] = jnp.concatenate(lines, axis=0)
    dot_copies = spread_out("anim", blocks, me, dots, dots, dot_send, dot_recv, False)
    arrive("anim", blocks, me, dots, dot_send, dot_recv)
    whole = dots[0]
    for b in range(1, blocks):
        whole = whole + dots[b]
    sums = jnp.sum(whole, axis=1, keepdims=True)
    old, curve, cross, image = (sums[i : i + 1] for i in range(4))
    step = old / curve
    new = old - 2.0 * step * cross + step * step * image
    coef_out[...] = jnp.broadcast_to(jnp.concatenate([step, new / old], axis=0), coef_out.shape)
    for copy in ghost_copies + marker_copies + back_copies + row_copies + dot_copies:
        copy.wait_send()


def update(
    image, coef, direction, residual, precondition, solution, new_solution, new_residual, new_direction
):
    step = coef[0:1, 0:1]
    ratio = coef[1:2, 0:1]
    for start in range(0, image.shape[1], STEP):
        at = slice(start, start + STEP)
        d = direction[:, at]
        left = residual[:, at] - step * image[:, at]
        pre = precondition[:, at]
        new_solution[:, at] = solution[:, at] + step * d
        new_residual[:, at] = left
        scaled = ratio * d
        new_direction[0:1, at] = pre[0:1] * left[0:1] + pre[1:2] * left[1:2] + scaled[0:1]
        new_direction[1:2, at] = pre[1:2] * left[0:1] + pre[2:3] * left[1:2] + scaled[1:2]


def on_device(
    blocks,
    layers,
    solution,
    residual,
    direction,
    record_inverse,
    precondition,
    genetic_inverse,
    sire_slot,
    dam_slot,
    send_rows,
    genotyped_row,
    genotypes,
    allele_freq,
    marker_weight,
):
    animals = direction.shape[1]
    rows = animals // LANES
    capacity = send_rows.shape[2]
    gen, markers = genotypes.shape
    chunk_rows = 256
    lists = (blocks, 2 * capacity // LANES, LANES)
    full_high = (animals + blocks * capacity) // WIDE
    vmem = pl.BlockSpec(memory_space=pltpu.VMEM)
    dma = pltpu.SemaphoreType.DMA
    f32 = jnp.float32
    pair = pltpu.VMEM((2, animals), f32)
    triple = pltpu.VMEM((3, animals), f32)
    hbm = lambda value: pltpu.with_memory_space_constraint(value, pltpu.HBM)
    carried = pl.pallas_call(
        functools.partial(kernel, blocks, layers),
        out_shape=(
            pair,
            pltpu.VMEM((2, LANES), f32),
            pair,
            pair,
            triple,
            pair,
        ),
        in_specs=[pl.BlockSpec(memory_space=pltpu.HBM)] * 16,
        out_specs=(vmem,) * 6,
        scratch_shapes=[
            pltpu.VMEM((3, animals), f32),
            pltpu.VMEM((2, 2), f32),
            pltpu.VMEM((rows, LANES), jnp.int32),
            pltpu.VMEM((rows, LANES), jnp.int32),
            pltpu.VMEM((1, animals), jnp.int32),
            pltpu.VMEM((1, animals), jnp.int32),
            pltpu.VMEM((blocks, capacity), jnp.int32),
            pltpu.VMEM((gen // LANES, LANES), jnp.int32),
            pltpu.VMEM((1, gen), jnp.int32),
            pltpu.VMEM((1, markers), f32),
            pltpu.VMEM((1, markers), f32),
            dma((15,)),
            pltpu.VMEM((gen // chunk_rows, chunk_rows, markers), jnp.int32),
            pltpu.VMEM((gen, markers), jnp.bfloat16),
            pltpu.VMEM((2, rows, LANES), f32),
            pltpu.VMEM(lists, f32),
            pltpu.VMEM(lists, f32),
            pltpu.VMEM(lists, f32),
            pltpu.VMEM(lists, f32),
            pltpu.VMEM((2, rows, LANES), f32),
            pltpu.VMEM((4 * full_high, WIDE), f32),
            pltpu.VMEM((2, animals // WIDE, WIDE), f32),
            pltpu.VMEM((blocks, 2, markers), f32),
            pltpu.VMEM((layers, 2, gen), f32),
            pltpu.VMEM((blocks, 8, LANES), f32),
            dma((gen // chunk_rows,)),
            dma((blocks - 1,)),
            dma((blocks,)),
            dma((blocks - 1,)),
            dma((blocks,)),
            dma((blocks - 1,)),
            dma((blocks,)),
            dma((layers - 1,)),
            dma((layers,)),
            dma((blocks - 1,)),
            dma((blocks,)),
        ],
        compiler_params=pltpu.CompilerParams(
            collective_id=0, has_side_effects=True, vmem_limit_bytes=50 * 2**20
        ),
    )(
        hbm(direction),
        hbm(residual),
        hbm(record_inverse),
        hbm(precondition),
        hbm(genetic_inverse),
        hbm(sire_slot.reshape(rows, LANES)),
        hbm(dam_slot.reshape(rows, LANES)),
        hbm(sire_slot.reshape(1, animals)),
        hbm(dam_slot.reshape(1, animals)),
        hbm(send_rows.reshape(blocks, capacity)),
        hbm(genotyped_row.reshape(gen // LANES, LANES)),
        hbm(genotyped_row.reshape(1, gen)),
        hbm(allele_freq.reshape(1, markers)),
        hbm(marker_weight.reshape(1, markers)),
        hbm(genotypes),
        hbm(solution),
    )
    return pl.pallas_call(
        update,
        out_shape=(jax.ShapeDtypeStruct((2, animals), f32),) * 3,
        in_specs=[vmem] * 6,
        out_specs=(vmem,) * 3,
    )(*carried)


def solution(mesh):
    return jax.shard_map(
        functools.partial(on_device, mesh.shape["anim"], mesh.shape["mark"]),
        mesh=mesh,
        in_specs=(
            P(None, "anim"),
            P(None, "anim"),
            P(None, "anim"),
            P(None, "anim"),
            P(None, "anim"),
            P(),
            P("anim"),
            P("anim"),
            P("anim", None, None),
            P("anim"),
            P("anim", "mark"),
            P("mark"),
            P("mark"),
        ),
        out_specs=(P(None, "anim"), P(None, "anim"), P(None, "anim")),
        check_vma=False,
    )
```

```python
import functools

import jax
import jax.numpy as jnp
from jax import lax
from jax.experimental import pallas as pl
from jax.experimental.pallas import tpu as pltpu
from jax.sharding import PartitionSpec as P

LANES = 128
WIDE = 256
STEP = 512
MESH = pl.DeviceIdType.MESH


def take(row, lane, like):
    table = jnp.broadcast_to(row, like.shape)
    return jnp.take_along_axis(table, lane, axis=1, mode="promise_in_bounds")


def split2(value):
    upper = value.astype(jnp.bfloat16).astype(jnp.float32)
    return upper, value - upper


def split3(value):
    upper, rest = split2(value)
    middle, lower = split2(rest)
    return upper, middle, lower


def scatter_product(index, values, height):
    high = index >> 8
    low = index & (WIDE - 1)
    count = index.shape[1]
    rows = lax.broadcasted_iota(jnp.int32, (height, count), 0) == high
    lanes = lax.broadcasted_iota(jnp.int32, (WIDE, count), 0) == low
    parts = []
    for value in values:
        for part in split2(value):
            parts.append(jnp.where(rows, part, 0.0).astype(jnp.bfloat16))
    left = jnp.concatenate(parts, axis=0)
    right = jnp.where(lanes, 1.0, 0.0).astype(jnp.bfloat16)
    return lax.dot_general(
        left, right, (((1,), (1,)), ((), ())), preferred_element_type=jnp.float32
    )


def kernel(
    blocks,
    layers,
    direction_hbm,
    residual_hbm,
    record_inverse_hbm,
    precondition_hbm,
    genetic_hbm,
    sire_hbm,
    dam_hbm,
    sire_flat_hbm,
    dam_flat_hbm,
    send_rows_hbm,
    picked_row_hbm,
    picked_flat_hbm,
    freq_hbm,
    weight_hbm,
    genotypes,
    solution_hbm,
    image_out,
    coef_out,
    direction,
    residual,
    precondition,
    solution,
    record_inverse,
    genetic,
    sire,
    dam,
    sire_flat,
    dam_flat,
    send_rows,
    picked_row,
    picked_flat,
    freq,
    weight,
    input_sem,
    codes,
    codes_half,
    table,
    outgoing,
    ghosts,
    outbound,
    inbound,
    parent,
    sampling,
    spread,
    gathered,
    marker_parts,
    row_parts,
    dots,
    code_sem,
    ghost_send,
    ghost_recv,
    back_send,
    back_recv,
    marker_send,
    marker_recv,
    row_send,
    row_recv,
    dot_send,
    dot_recv,
):
    animals = direction.shape[1]
    rows = animals // LANES
    capacity = send_rows.shape[1]
    spots = capacity // LANES
    gen_rows = picked_row.shape[0]
    markers = freq.shape[1]
    local_high = animals // WIDE
    full_high = local_high + blocks * capacity // WIDE
    chunks = codes.shape[0]
    chunk_rows = codes.shape[1]
    me = lax.axis_index("anim")
    layer = lax.axis_index("mark")

    def fetch(c):
        return pltpu.make_async_copy(
            genotypes.at[pl.ds(c * chunk_rows, chunk_rows)], codes.at[c], code_sem.at[c]
        )

    loads = [
        pltpu.make_async_copy(source, target, input_sem.at[i])
        for i, (source, target) in enumerate(
            [
                (direction_hbm, direction),
                (send_rows_hbm, send_rows),
                (picked_row_hbm, picked_row),
                (freq_hbm, freq),
                (sire_hbm, sire),
                (dam_hbm, dam),
                (sire_flat_hbm, sire_flat),
                (dam_flat_hbm, dam_flat),
                (weight_hbm, weight),
                (picked_flat_hbm, picked_flat),
                (genetic_hbm, genetic),
                (record_inverse_hbm, record_inverse),
                (residual_hbm, residual),
                (precondition_hbm, precondition),
                (solution_hbm, solution),
            ]
        )
    ]
    for load in loads[:4]:
        load.start()
    for c in range(chunks):
        fetch(c).start()
    for load in loads[4:]:
        load.start()

    barrier = pltpu.get_barrier_semaphore()
    for off in range(1, blocks):
        pl.semaphore_signal(
            barrier, inc=1, device_id={"anim": lax.rem(me + off, blocks)}, device_id_type=MESH
        )
    for off in range(1, layers):
        pl.semaphore_signal(
            barrier, inc=1, device_id={"mark": lax.rem(layer + off, layers)}, device_id_type=MESH
        )

    def spread_out(axis, size, mine, buffer_from, buffer_to, send_sem, recv_sem, by_target):
        copies = []
        for off in range(1, size):
            peer = lax.rem(mine + off, size)
            copy = pltpu.make_async_remote_copy(
                src_ref=buffer_from.at[peer] if by_target else buffer_from.at[mine],
                dst_ref=buffer_to.at[mine],
                send_sem=send_sem.at[off - 1],
                recv_sem=recv_sem.at[mine],
                device_id={axis: peer},
                device_id_type=MESH,
            )
            copy.start()
            copies.append(copy)
        return copies

    def arrive(axis, size, mine, buffer, send_sem, recv_sem):
        for off in range(1, size):
            peer = lax.rem(mine + off, size)
            pltpu.make_async_remote_copy(
                src_ref=buffer.at[peer],
                dst_ref=buffer.at[peer],
                send_sem=send_sem.at[off - 1],
                recv_sem=recv_sem.at[peer],
                device_id={axis: peer},
                device_id_type=MESH,
            ).wait_recv()

    for load in loads[:3]:
        load.wait()
    for r in range(rows):
        pair = direction[:, r * LANES : (r + 1) * LANES]
        table[0, r : r + 1, :] = pair[0:1]
        table[1, r : r + 1, :] = pair[1:2]

    wanted = [send_rows[:, k * LANES : (k + 1) * LANES] for k in range(spots)]
    wanted.append(picked_row[...])
    found = []
    for index in wanted:
        high, lane = index >> 7, index & (LANES - 1)
        values = [jnp.zeros(index.shape, jnp.float32)] * 2
        for r in range(rows):
            here = high == r
            values = [
                jnp.where(here, take(table[t, r : r + 1, :], lane, lane), values[t])
                for t in range(2)
            ]
        found.append(values)
    for k in range(spots):
        for trait in range(2):
            for b in range(blocks):
                outgoing[b, trait * spots + k : trait * spots + k + 1, :] = found[k][trait][b : b + 1]
    picked = found[spots]

    pl.semaphore_wait(barrier, blocks - 1 + layers - 1)
    ghost_copies = spread_out("anim", blocks, me, outgoing, ghosts, ghost_send, ghost_recv, True)
    ghosts[me] = jnp.zeros(ghosts.shape[1:], jnp.float32)

    picked_parts = [split3(value) for value in picked]
    total = jnp.zeros((6, markers), jnp.float32)
    per_chunk = chunk_rows // LANES
    for c in range(chunks):
        fetch(c).wait()
        codes_half[pl.ds(c * chunk_rows, chunk_rows), :] = (
            codes[c].astype(jnp.float32).astype(jnp.bfloat16)
        )
        lines = []
        for part in range(3):
            for trait in range(2):
                block = picked_parts[trait][part]
                lines.append(
                    jnp.concatenate(
                        [block[c * per_chunk + i : c * per_chunk + i + 1] for i in range(per_chunk)],
                        axis=1,
                    )
                )
        left = jnp.concatenate(lines, axis=0).astype(jnp.bfloat16)
        total = total + jnp.dot(
            left,
            codes_half[pl.ds(c * chunk_rows, chunk_rows), :],
            preferred_element_type=jnp.float32,
        )
    loads[3].wait()
    frequency = 2.0 * freq[...]
    sums = [jnp.sum(picked[trait]) for trait in range(2)]
    marker_parts[me] = jnp.concatenate(
        [
            (total[t : t + 1] + total[2 + t : 3 + t] + total[4 + t : 5 + t]) - sums[t] * frequency
            for t in range(2)
        ],
        axis=0,
    )
    marker_copies = spread_out(
        "anim", blocks, me, marker_parts, marker_parts, marker_send, marker_recv, False
    )

    for load in loads[4:8]:
        load.wait()
    slots = [sire[...], dam[...]]
    known = (slots[0] >= 0).astype(jnp.float32) + (slots[1] >= 0).astype(jnp.float32)
    group = 8

    def local(i, carry):
        at = pl.ds(pl.multiple_of(i * group, group), group)
        for which, slot in enumerate((sire, dam)):
            index = slot[at]
            high, lane = index >> 7, index & (LANES - 1)
            found = [jnp.zeros(index.shape, jnp.float32)] * 2
            for r in range(rows):
                here = high == r
                found = [
                    jnp.where(here, take(table[t, r : r + 1, :], lane, lane), found[t])
                    for t in range(2)
                ]
            for t in range(2):
                parent[which, t, at] = found[t]
        return carry

    lax.fori_loop(0, rows // group, local, 0)
    arrive("anim", blocks, me, ghosts, ghost_send, ghost_recv)

    def remote(i, carry):
        at = pl.ds(pl.multiple_of(i * group, group), group)
        for which, slot in enumerate((sire, dam)):
            index = slot[at]
            high, lane = index >> 7, index & (LANES - 1)
            found = [parent[which, t, at] for t in range(2)]
            for source in range(blocks):
                for k in range(spots):
                    here = high == rows + source * spots + k
                    found = [
                        jnp.where(
                            here,
                            take(ghosts[source, t * spots + k : t * spots + k + 1, :], lane, lane),
                            found[t],
                        )
                        for t in range(2)
                    ]
            for t in range(2):
                parent[which, t, at] = found[t]
        return carry

    lax.fori_loop(0, rows // group, remote, 0)
    factor = 1.0 / (1.0 - 0.25 * known)
    for t in range(2):
        sampling[t] = factor * (table[t] - 0.5 * (parent[0, t] + parent[1, t]))

    spread[...] = jnp.zeros(spread.shape, jnp.float32)
    lines_per_step = STEP // LANES

    def sampling_lines(t, j):
        return jnp.concatenate(
            [sampling[t, pl.ds(j * lines_per_step + i, 1), :] for i in range(lines_per_step)], axis=1
        )

    def offspring(j, carry):
        values = [-0.5 * sampling_lines(t, j) for t in range(2)]
        at = pl.ds(pl.multiple_of(j * STEP, STEP), STEP)
        spread[...] += scatter_product(sire_flat[:, at], values, full_high) + scatter_product(
            dam_flat[:, at], values, full_high
        )
        return carry

    lax.fori_loop(0, animals // STEP, offspring, 0)
    per_source = capacity // WIDE
    for t in range(2):
        both = spread[2 * t * full_high : (2 * t + 1) * full_high] + spread[
            (2 * t + 1) * full_high : (2 * t + 2) * full_high
        ]
        gathered[t] = both[:local_high]
        for b in range(blocks):
            for i in range(per_source):
                h = local_high + b * per_source + i
                for half in range(2):
                    at = t * spots + 2 * i + half
                    outbound[b, at : at + 1, :] = both[h : h + 1, half * LANES : (half + 1) * LANES]
    back_copies = spread_out("anim", blocks, me, outbound, inbound, back_send, back_recv, True)
    inbound[me] = jnp.zeros(inbound.shape[1:], jnp.float32)

    arrive("anim", blocks, me, marker_parts, marker_send, marker_recv)
    loads[8].wait()
    marker_total = marker_parts[0]
    for b in range(1, blocks):
        marker_total = marker_total + marker_parts[b]
    scaled = marker_total * weight[...] / (markers * layers)
    offset = jnp.sum(scaled * frequency, axis=1, keepdims=True)
    left = jnp.concatenate(split3(scaled), axis=0).astype(jnp.bfloat16)
    row_sums = lax.dot_general(
        left, codes_half[...], (((1,), (1,)), ((), ())), preferred_element_type=jnp.float32
    )
    row_parts[layer] = row_sums[0:2] + row_sums[2:4] + row_sums[4:6] - offset
    row_copies = spread_out("mark", layers, layer, row_parts, row_parts, row_send, row_recv, False)

    arrive("anim", blocks, me, inbound, back_send, back_recv)

    def returned(b, carry):
        values = [
            jnp.concatenate(
                [inbound[b, t * spots + k : t * spots + k + 1, :] for k in range(spots)], axis=1
            )
            for t in range(2)
        ]
        return carry + scatter_product(send_rows[pl.ds(b, 1), :], values, local_high)

    added = lax.fori_loop(0, blocks, returned, jnp.zeros((4 * local_high, WIDE), jnp.float32))
    for load in loads[9:]:
        load.wait()
    arrive("mark", layers, layer, row_parts, row_send, row_recv)
    genomic = row_parts[0]
    for z in range(1, layers):
        genomic = genomic + row_parts[z]
    added = added + scatter_product(picked_flat[...], [genomic[0:1], genomic[1:2]], local_high)
    for t in range(2):
        gathered[t] = (
            gathered[t]
            + added[2 * t * local_high : (2 * t + 1) * local_high]
            + added[(2 * t + 1) * local_high : (2 * t + 2) * local_high]
        )

    g00, g01, g10, g11 = (genetic[a : a + 1, b : b + 1] for a in range(2) for b in range(2))

    def finish(j, carry):
        at = pl.ds(pl.multiple_of(j * STEP, STEP), STEP)
        d = direction[:, at]
        r = residual[:, at]
        rec = record_inverse[:, at]
        pre = precondition[:, at]
        d0, d1, r0, r1 = d[0:1], d[1:2], r[0:1], r[1:2]
        terms = [
            sampling_lines(t, j)
            + jnp.concatenate(
                [gathered[t, pl.ds(j * (STEP // WIDE) + i, 1), :] for i in range(STEP // WIDE)],
                axis=1,
            )
            for t in range(2)
        ]
        i0 = rec[0:1] * d0 + rec[1:2] * d1 + (g00 * terms[0] + g01 * terms[1])
        i1 = rec[1:2] * d0 + rec[2:3] * d1 + (g10 * terms[0] + g11 * terms[1])
        image_out[0:1, at] = i0
        image_out[1:2, at] = i1
        s0 = pre[0:1] * r0 + pre[1:2] * r1
        s1 = pre[1:2] * r0 + pre[2:3] * r1
        m0 = pre[0:1] * i0 + pre[1:2] * i1
        m1 = pre[1:2] * i0 + pre[2:3] * i1
        old, curve, cross, image = carry
        return (
            old + (r0 * s0 + r1 * s1),
            curve + (d0 * i0 + d1 * i1),
            cross + (i0 * s0 + i1 * s1),
            image + (i0 * m0 + i1 * m1),
        )

    zero = jnp.zeros((1, STEP), jnp.float32)
    products = lax.fori_loop(0, animals // STEP, finish, (zero,) * 4)
    lines = [
        sum(value[:, i * LANES : (i + 1) * LANES] for i in range(STEP // LANES))
        for value in products
    ]
    lines.append(jnp.zeros((4, LANES), jnp.float32))
    dots[me] = jnp.concatenate(lines, axis=0)
    dot_copies = spread_out("anim", blocks, me, dots, dots, dot_send, dot_recv, False)
    arrive("anim", blocks, me, dots, dot_send, dot_recv)
    whole = dots[0]
    for b in range(1, blocks):
        whole = whole + dots[b]
    sums = jnp.sum(whole, axis=1, keepdims=True)
    old, curve, cross, image = (sums[i : i + 1] for i in range(4))
    step = old / curve
    new = old - 2.0 * step * cross + step * step * image
    coef_out[...] = jnp.broadcast_to(jnp.concatenate([step, new / old], axis=0), coef_out.shape)
    for copy in ghost_copies + marker_copies + back_copies + row_copies + dot_copies:
        copy.wait_send()


def update(
    image, coef, direction, residual, precondition, solution, new_solution, new_residual, new_direction
):
    step = coef[0:1, 0:1]
    ratio = coef[1:2, 0:1]
    for start in range(0, image.shape[1], STEP):
        at = slice(start, start + STEP)
        d = direction[:, at]
        left = residual[:, at] - step * image[:, at]
        pre = precondition[:, at]
        new_solution[:, at] = solution[:, at] + step * d
        new_residual[:, at] = left
        scaled = ratio * d
        new_direction[0:1, at] = pre[0:1] * left[0:1] + pre[1:2] * left[1:2] + scaled[0:1]
        new_direction[1:2, at] = pre[1:2] * left[0:1] + pre[2:3] * left[1:2] + scaled[1:2]


def on_device(
    blocks,
    layers,
    solution,
    residual,
    direction,
    record_inverse,
    precondition,
    genetic_inverse,
    sire_slot,
    dam_slot,
    send_rows,
    genotyped_row,
    genotypes,
    allele_freq,
    marker_weight,
):
    animals = direction.shape[1]
    rows = animals // LANES
    capacity = send_rows.shape[2]
    gen, markers = genotypes.shape
    chunk_rows = 256
    lists = (blocks, 2 * capacity // LANES, LANES)
    full_high = (animals + blocks * capacity) // WIDE
    vmem = pl.BlockSpec(memory_space=pltpu.VMEM)
    dma = pltpu.SemaphoreType.DMA
    f32 = jnp.float32
    pair = pltpu.VMEM((2, animals), f32)
    triple = pltpu.VMEM((3, animals), f32)
    hbm = lambda value: pltpu.with_memory_space_constraint(value, pltpu.HBM)
    carried = pl.pallas_call(
        functools.partial(kernel, blocks, layers),
        out_shape=(
            pair,
            pltpu.VMEM((2, LANES), f32),
            pair,
            pair,
            triple,
            pair,
        ),
        in_specs=[pl.BlockSpec(memory_space=pltpu.HBM)] * 16,
        out_specs=(vmem,) * 6,
        scratch_shapes=[
            pltpu.VMEM((3, animals), f32),
            pltpu.VMEM((2, 2), f32),
            pltpu.VMEM((rows, LANES), jnp.int32),
            pltpu.VMEM((rows, LANES), jnp.int32),
            pltpu.VMEM((1, animals), jnp.int32),
            pltpu.VMEM((1, animals), jnp.int32),
            pltpu.VMEM((blocks, capacity), jnp.int32),
            pltpu.VMEM((gen // LANES, LANES), jnp.int32),
            pltpu.VMEM((1, gen), jnp.int32),
            pltpu.VMEM((1, markers), f32),
            pltpu.VMEM((1, markers), f32),
            dma((15,)),
            pltpu.VMEM((gen // chunk_rows, chunk_rows, markers), jnp.int32),
            pltpu.VMEM((gen, markers), jnp.bfloat16),
            pltpu.VMEM((2, rows, LANES), f32),
            pltpu.VMEM(lists, f32),
            pltpu.VMEM(lists, f32),
            pltpu.VMEM(lists, f32),
            pltpu.VMEM(lists, f32),
            pltpu.VMEM((2, 2, rows, LANES), f32),
            pltpu.VMEM((2, rows, LANES), f32),
            pltpu.VMEM((4 * full_high, WIDE), f32),
            pltpu.VMEM((2, animals // WIDE, WIDE), f32),
            pltpu.VMEM((blocks, 2, markers), f32),
            pltpu.VMEM((layers, 2, gen), f32),
            pltpu.VMEM((blocks, 8, LANES), f32),
            dma((gen // chunk_rows,)),
            dma((blocks - 1,)),
            dma((blocks,)),
            dma((blocks - 1,)),
            dma((blocks,)),
            dma((blocks - 1,)),
            dma((blocks,)),
            dma((layers - 1,)),
            dma((layers,)),
            dma((blocks - 1,)),
            dma((blocks,)),
        ],
        compiler_params=pltpu.CompilerParams(
            collective_id=0, has_side_effects=True, vmem_limit_bytes=50 * 2**20
        ),
    )(
        hbm(direction),
        hbm(residual),
        hbm(record_inverse),
        hbm(precondition),
        hbm(genetic_inverse),
        hbm(sire_slot.reshape(rows, LANES)),
        hbm(dam_slot.reshape(rows, LANES)),
        hbm(sire_slot.reshape(1, animals)),
        hbm(dam_slot.reshape(1, animals)),
        hbm(send_rows.reshape(blocks, capacity)),
        hbm(genotyped_row.reshape(gen // LANES, LANES)),
        hbm(genotyped_row.reshape(1, gen)),
        hbm(allele_freq.reshape(1, markers)),
        hbm(marker_weight.reshape(1, markers)),
        hbm(genotypes),
        hbm(solution),
    )
    return pl.pallas_call(
        update,
        out_shape=(jax.ShapeDtypeStruct((2, animals), f32),) * 3,
        in_specs=[vmem] * 6,
        out_specs=(vmem,) * 3,
        compiler_params=pltpu.CompilerParams(vmem_limit_bytes=8 * 2**20),
    )(*[pltpu.with_memory_space_constraint(value, pltpu.VMEM) for value in carried])


def solution(mesh):
    return jax.shard_map(
        functools.partial(on_device, mesh.shape["anim"], mesh.shape["mark"]),
        mesh=mesh,
        in_specs=(
            P(None, "anim"),
            P(None, "anim"),
            P(None, "anim"),
            P(None, "anim"),
            P(None, "anim"),
            P(),
            P("anim"),
            P("anim"),
            P("anim", None, None),
            P("anim"),
            P("anim", "mark"),
            P("mark"),
            P("mark"),
        ),
        out_specs=(P(None, "anim"), P(None, "anim"), P(None, "anim")),
        check_vma=False,
    )
```

```python
import functools

import jax
import jax.numpy as jnp
from jax import lax
from jax.experimental import pallas as pl
from jax.experimental.pallas import tpu as pltpu
from jax.sharding import PartitionSpec as P

LANES = 128
WIDE = 256
STEP = 2048
MESH = pl.DeviceIdType.MESH


def take(row, lane, like):
    table = jnp.broadcast_to(row, like.shape)
    return jnp.take_along_axis(table, lane, axis=1, mode="promise_in_bounds")


def split2(value):
    upper = value.astype(jnp.bfloat16).astype(jnp.float32)
    return upper, value - upper


def split3(value):
    upper, rest = split2(value)
    middle, lower = split2(rest)
    return upper, middle, lower


def scatter_product(index, values, height):
    high = index >> 8
    low = index & (WIDE - 1)
    count = index.shape[1]
    rows = lax.broadcasted_iota(jnp.int32, (height, count), 0) == high
    lanes = lax.broadcasted_iota(jnp.int32, (WIDE, count), 0) == low
    parts = []
    for value in values:
        for part in split2(value):
            parts.append(jnp.where(rows, part, 0.0).astype(jnp.bfloat16))
    left = jnp.concatenate(parts, axis=0)
    right = jnp.where(lanes, 1.0, 0.0).astype(jnp.bfloat16)
    return lax.dot_general(
        left, right, (((1,), (1,)), ((), ())), preferred_element_type=jnp.float32
    )


def kernel(
    blocks,
    layers,
    direction_hbm,
    residual_hbm,
    record_inverse_hbm,
    precondition_hbm,
    genetic_hbm,
    sire_hbm,
    dam_hbm,
    sire_flat_hbm,
    dam_flat_hbm,
    send_rows_hbm,
    picked_row_hbm,
    picked_flat_hbm,
    freq_hbm,
    weight_hbm,
    genotypes,
    solution_hbm,
    image_out,
    coef_out,
    direction,
    residual,
    precondition,
    solution,
    record_inverse,
    genetic,
    sire,
    dam,
    sire_flat,
    dam_flat,
    send_rows,
    picked_row,
    picked_flat,
    freq,
    weight,
    input_sem,
    codes,
    codes_half,
    table,
    outgoing,
    ghosts,
    outbound,
    inbound,
    parent,
    sampling,
    spread,
    gathered,
    marker_parts,
    row_parts,
    dots,
    code_sem,
    ghost_send,
    ghost_recv,
    back_send,
    back_recv,
    marker_send,
    marker_recv,
    row_send,
    row_recv,
    dot_send,
    dot_recv,
):
    animals = direction.shape[1]
    rows = animals // LANES
    capacity = send_rows.shape[1]
    spots = capacity // LANES
    gen_rows = picked_row.shape[0]
    markers = freq.shape[1]
    local_high = animals // WIDE
    full_high = local_high + blocks * capacity // WIDE
    chunks = codes.shape[0]
    chunk_rows = codes.shape[1]
    me = lax.axis_index("anim")
    layer = lax.axis_index("mark")

    def fetch(c):
        return pltpu.make_async_copy(
            genotypes.at[pl.ds(c * chunk_rows, chunk_rows)], codes.at[c], code_sem.at[c]
        )

    loads = [
        pltpu.make_async_copy(source, target, input_sem.at[i])
        for i, (source, target) in enumerate(
            [
                (direction_hbm, direction),
                (send_rows_hbm, send_rows),
                (picked_row_hbm, picked_row),
                (freq_hbm, freq),
                (sire_hbm, sire),
                (dam_hbm, dam),
                (sire_flat_hbm, sire_flat),
                (dam_flat_hbm, dam_flat),
                (weight_hbm, weight),
                (picked_flat_hbm, picked_flat),
                (genetic_hbm, genetic),
                (record_inverse_hbm, record_inverse),
                (residual_hbm, residual),
                (precondition_hbm, precondition),
                (solution_hbm, solution),
            ]
        )
    ]
    for load in loads[:4]:
        load.start()
    for c in range(chunks):
        fetch(c).start()
    for load in loads[4:]:
        load.start()

    barrier = pltpu.get_barrier_semaphore()
    for off in range(1, blocks):
        pl.semaphore_signal(
            barrier, inc=1, device_id={"anim": lax.rem(me + off, blocks)}, device_id_type=MESH
        )
    for off in range(1, layers):
        pl.semaphore_signal(
            barrier, inc=1, device_id={"mark": lax.rem(layer + off, layers)}, device_id_type=MESH
        )

    def spread_out(axis, size, mine, buffer_from, buffer_to, send_sem, recv_sem, by_target):
        copies = []
        for off in range(1, size):
            peer = lax.rem(mine + off, size)
            copy = pltpu.make_async_remote_copy(
                src_ref=buffer_from.at[peer] if by_target else buffer_from.at[mine],
                dst_ref=buffer_to.at[mine],
                send_sem=send_sem.at[off - 1],
                recv_sem=recv_sem.at[mine],
                device_id={axis: peer},
                device_id_type=MESH,
            )
            copy.start()
            copies.append(copy)
        return copies

    def arrive(axis, size, mine, buffer, send_sem, recv_sem):
        for off in range(1, size):
            peer = lax.rem(mine + off, size)
            pltpu.make_async_remote_copy(
                src_ref=buffer.at[peer],
                dst_ref=buffer.at[peer],
                send_sem=send_sem.at[off - 1],
                recv_sem=recv_sem.at[peer],
                device_id={axis: peer},
                device_id_type=MESH,
            ).wait_recv()

    for load in loads[:3]:
        load.wait()
    for r in range(rows):
        pair = direction[:, r * LANES : (r + 1) * LANES]
        table[0, r : r + 1, :] = pair[0:1]
        table[1, r : r + 1, :] = pair[1:2]

    wanted = [send_rows[:, k * LANES : (k + 1) * LANES] for k in range(spots)]
    wanted.append(picked_row[...])
    found = []
    for index in wanted:
        high, lane = index >> 7, index & (LANES - 1)
        values = [jnp.zeros(index.shape, jnp.float32)] * 2
        for r in range(rows):
            here = high == r
            values = [
                jnp.where(here, take(table[t, r : r + 1, :], lane, lane), values[t])
                for t in range(2)
            ]
        found.append(values)
    for k in range(spots):
        for trait in range(2):
            for b in range(blocks):
                outgoing[b, trait * spots + k : trait * spots + k + 1, :] = found[k][trait][b : b + 1]
    picked = found[spots]

    pl.semaphore_wait(barrier, blocks - 1 + layers - 1)
    ghost_copies = spread_out("anim", blocks, me, outgoing, ghosts, ghost_send, ghost_recv, True)
    ghosts[me] = jnp.zeros(ghosts.shape[1:], jnp.float32)

    picked_parts = [split3(value) for value in picked]
    total = jnp.zeros((6, markers), jnp.float32)
    per_chunk = chunk_rows // LANES
    for c in range(chunks):
        fetch(c).wait()
        codes_half[pl.ds(c * chunk_rows, chunk_rows), :] = (
            codes[c].astype(jnp.float32).astype(jnp.bfloat16)
        )
        lines = []
        for part in range(3):
            for trait in range(2):
                block = picked_parts[trait][part]
                lines.append(
                    jnp.concatenate(
                        [block[c * per_chunk + i : c * per_chunk + i + 1] for i in range(per_chunk)],
                        axis=1,
                    )
                )
        left = jnp.concatenate(lines, axis=0).astype(jnp.bfloat16)
        total = total + jnp.dot(
            left,
            codes_half[pl.ds(c * chunk_rows, chunk_rows), :],
            preferred_element_type=jnp.float32,
        )
    loads[3].wait()
    frequency = 2.0 * freq[...]
    sums = [jnp.sum(picked[trait]) for trait in range(2)]
    marker_parts[me] = jnp.concatenate(
        [
            (total[t : t + 1] + total[2 + t : 3 + t] + total[4 + t : 5 + t]) - sums[t] * frequency
            for t in range(2)
        ],
        axis=0,
    )
    marker_copies = spread_out(
        "anim", blocks, me, marker_parts, marker_parts, marker_send, marker_recv, False
    )

    for load in loads[4:8]:
        load.wait()
    slots = [sire[...], dam[...]]
    known = (slots[0] >= 0).astype(jnp.float32) + (slots[1] >= 0).astype(jnp.float32)
    group = 8

    def local(i, carry):
        at = pl.ds(pl.multiple_of(i * group, group), group)
        for which, slot in enumerate((sire, dam)):
            index = slot[at]
            high, lane = index >> 7, index & (LANES - 1)
            found = [jnp.zeros(index.shape, jnp.float32)] * 2
            for r in range(rows):
                here = high == r
                found = [
                    jnp.where(here, take(table[t, r : r + 1, :], lane, lane), found[t])
                    for t in range(2)
                ]
            for t in range(2):
                parent[which, t, at] = found[t]
        return carry

    lax.fori_loop(0, rows // group, local, 0)
    arrive("anim", blocks, me, ghosts, ghost_send, ghost_recv)

    def remote(i, carry):
        at = pl.ds(pl.multiple_of(i * group, group), group)
        for which, slot in enumerate((sire, dam)):
            index = slot[at]
            high, lane = index >> 7, index & (LANES - 1)
            found = [parent[which, t, at] for t in range(2)]
            for source in range(blocks):
                for k in range(spots):
                    here = high == rows + source * spots + k
                    found = [
                        jnp.where(
                            here,
                            take(ghosts[source, t * spots + k : t * spots + k + 1, :], lane, lane),
                            found[t],
                        )
                        for t in range(2)
                    ]
            for t in range(2):
                parent[which, t, at] = found[t]
        return carry

    lax.fori_loop(0, rows // group, remote, 0)
    factor = 1.0 / (1.0 - 0.25 * known)
    for t in range(2):
        sampling[t] = factor * (table[t] - 0.5 * (parent[0, t] + parent[1, t]))

    spread[...] = jnp.zeros(spread.shape, jnp.float32)
    lines_per_step = STEP // LANES

    def sampling_lines(t, j):
        return jnp.concatenate(
            [sampling[t, pl.ds(j * lines_per_step + i, 1), :] for i in range(lines_per_step)], axis=1
        )

    def offspring(j, carry):
        values = [-0.5 * sampling_lines(t, j) for t in range(2)]
        at = pl.ds(pl.multiple_of(j * STEP, STEP), STEP)
        spread[...] += scatter_product(sire_flat[:, at], values, full_high) + scatter_product(
            dam_flat[:, at], values, full_high
        )
        return carry

    lax.fori_loop(0, animals // STEP, offspring, 0)
    per_source = capacity // WIDE
    for t in range(2):
        both = spread[2 * t * full_high : (2 * t + 1) * full_high] + spread[
            (2 * t + 1) * full_high : (2 * t + 2) * full_high
        ]
        gathered[t] = both[:local_high]
        for b in range(blocks):
            for i in range(per_source):
                h = local_high + b * per_source + i
                for half in range(2):
                    at = t * spots + 2 * i + half
                    outbound[b, at : at + 1, :] = both[h : h + 1, half * LANES : (half + 1) * LANES]
    back_copies = spread_out("anim", blocks, me, outbound, inbound, back_send, back_recv, True)
    inbound[me] = jnp.zeros(inbound.shape[1:], jnp.float32)

    arrive("anim", blocks, me, marker_parts, marker_send, marker_recv)
    loads[8].wait()
    marker_total = marker_parts[0]
    for b in range(1, blocks):
        marker_total = marker_total + marker_parts[b]
    scaled = marker_total * weight[...] / (markers * layers)
    offset = jnp.sum(scaled * frequency, axis=1, keepdims=True)
    left = jnp.concatenate(split3(scaled), axis=0).astype(jnp.bfloat16)
    row_sums = lax.dot_general(
        left, codes_half[...], (((1,), (1,)), ((), ())), preferred_element_type=jnp.float32
    )
    row_parts[layer] = row_sums[0:2] + row_sums[2:4] + row_sums[4:6] - offset
    row_copies = spread_out("mark", layers, layer, row_parts, row_parts, row_send, row_recv, False)

    arrive("anim", blocks, me, inbound, back_send, back_recv)

    def returned(b, carry):
        values = [
            jnp.concatenate(
                [inbound[b, t * spots + k : t * spots + k + 1, :] for k in range(spots)], axis=1
            )
            for t in range(2)
        ]
        return carry + scatter_product(send_rows[pl.ds(b, 1), :], values, local_high)

    added = lax.fori_loop(0, blocks, returned, jnp.zeros((4 * local_high, WIDE), jnp.float32))
    for load in loads[9:]:
        load.wait()
    arrive("mark", layers, layer, row_parts, row_send, row_recv)
    genomic = row_parts[0]
    for z in range(1, layers):
        genomic = genomic + row_parts[z]
    added = added + scatter_product(picked_flat[...], [genomic[0:1], genomic[1:2]], local_high)
    for t in range(2):
        gathered[t] = (
            gathered[t]
            + added[2 * t * local_high : (2 * t + 1) * local_high]
            + added[(2 * t + 1) * local_high : (2 * t + 2) * local_high]
        )

    g00, g01, g10, g11 = (genetic[a : a + 1, b : b + 1] for a in range(2) for b in range(2))

    def finish(j, carry):
        at = pl.ds(pl.multiple_of(j * STEP, STEP), STEP)
        d = direction[:, at]
        r = residual[:, at]
        rec = record_inverse[:, at]
        pre = precondition[:, at]
        d0, d1, r0, r1 = d[0:1], d[1:2], r[0:1], r[1:2]
        terms = [
            sampling_lines(t, j)
            + jnp.concatenate(
                [gathered[t, pl.ds(j * (STEP // WIDE) + i, 1), :] for i in range(STEP // WIDE)],
                axis=1,
            )
            for t in range(2)
        ]
        i0 = rec[0:1] * d0 + rec[1:2] * d1 + (g00 * terms[0] + g01 * terms[1])
        i1 = rec[1:2] * d0 + rec[2:3] * d1 + (g10 * terms[0] + g11 * terms[1])
        image_out[0:1, at] = i0
        image_out[1:2, at] = i1
        s0 = pre[0:1] * r0 + pre[1:2] * r1
        s1 = pre[1:2] * r0 + pre[2:3] * r1
        m0 = pre[0:1] * i0 + pre[1:2] * i1
        m1 = pre[1:2] * i0 + pre[2:3] * i1
        old, curve, cross, image = carry
        return (
            old + (r0 * s0 + r1 * s1),
            curve + (d0 * i0 + d1 * i1),
            cross + (i0 * s0 + i1 * s1),
            image + (i0 * m0 + i1 * m1),
        )

    zero = jnp.zeros((1, STEP), jnp.float32)
    products = lax.fori_loop(0, animals // STEP, finish, (zero,) * 4)
    lines = [
        sum(value[:, i * LANES : (i + 1) * LANES] for i in range(STEP // LANES))
        for value in products
    ]
    lines.append(jnp.zeros((4, LANES), jnp.float32))
    dots[me] = jnp.concatenate(lines, axis=0)
    dot_copies = spread_out("anim", blocks, me, dots, dots, dot_send, dot_recv, False)
    arrive("anim", blocks, me, dots, dot_send, dot_recv)
    whole = dots[0]
    for b in range(1, blocks):
        whole = whole + dots[b]
    sums = jnp.sum(whole, axis=1, keepdims=True)
    old, curve, cross, image = (sums[i : i + 1] for i in range(4))
    step = old / curve
    new = old - 2.0 * step * cross + step * step * image
    coef_out[...] = jnp.broadcast_to(jnp.concatenate([step, new / old], axis=0), coef_out.shape)
    for copy in ghost_copies + marker_copies + back_copies + row_copies + dot_copies:
        copy.wait_send()


def update(
    image, coef, direction, residual, precondition, solution, new_solution, new_residual, new_direction
):
    step = coef[0:1, 0:1]
    ratio = coef[1:2, 0:1]
    for start in range(0, image.shape[1], STEP):
        at = slice(start, start + STEP)
        d = direction[:, at]
        left = residual[:, at] - step * image[:, at]
        pre = precondition[:, at]
        new_solution[:, at] = solution[:, at] + step * d
        new_residual[:, at] = left
        scaled = ratio * d
        new_direction[0:1, at] = pre[0:1] * left[0:1] + pre[1:2] * left[1:2] + scaled[0:1]
        new_direction[1:2, at] = pre[1:2] * left[0:1] + pre[2:3] * left[1:2] + scaled[1:2]


def on_device(
    blocks,
    layers,
    solution,
    residual,
    direction,
    record_inverse,
    precondition,
    genetic_inverse,
    sire_slot,
    dam_slot,
    send_rows,
    genotyped_row,
    genotypes,
    allele_freq,
    marker_weight,
):
    animals = direction.shape[1]
    rows = animals // LANES
    capacity = send_rows.shape[2]
    gen, markers = genotypes.shape
    chunk_rows = 256
    lists = (blocks, 2 * capacity // LANES, LANES)
    full_high = (animals + blocks * capacity) // WIDE
    vmem = pl.BlockSpec(memory_space=pltpu.VMEM)
    dma = pltpu.SemaphoreType.DMA
    f32 = jnp.float32
    pair = pltpu.VMEM((2, animals), f32)
    triple = pltpu.VMEM((3, animals), f32)
    hbm = lambda value: pltpu.with_memory_space_constraint(value, pltpu.HBM)
    carried = pl.pallas_call(
        functools.partial(kernel, blocks, layers),
        out_shape=(
            pair,
            pltpu.VMEM((2, LANES), f32),
            pair,
            pair,
            triple,
            pair,
        ),
        in_specs=[pl.BlockSpec(memory_space=pltpu.HBM)] * 16,
        out_specs=(vmem,) * 6,
        scratch_shapes=[
            pltpu.VMEM((3, animals), f32),
            pltpu.VMEM((2, 2), f32),
            pltpu.VMEM((rows, LANES), jnp.int32),
            pltpu.VMEM((rows, LANES), jnp.int32),
            pltpu.VMEM((1, animals), jnp.int32),
            pltpu.VMEM((1, animals), jnp.int32),
            pltpu.VMEM((blocks, capacity), jnp.int32),
            pltpu.VMEM((gen // LANES, LANES), jnp.int32),
            pltpu.VMEM((1, gen), jnp.int32),
            pltpu.VMEM((1, markers), f32),
            pltpu.VMEM((1, markers), f32),
            dma((15,)),
            pltpu.VMEM((gen // chunk_rows, chunk_rows, markers), jnp.int32),
            pltpu.VMEM((gen, markers), jnp.bfloat16),
            pltpu.VMEM((2, rows, LANES), f32),
            pltpu.VMEM(lists, f32),
            pltpu.VMEM(lists, f32),
            pltpu.VMEM(lists, f32),
            pltpu.VMEM(lists, f32),
            pltpu.VMEM((2, 2, rows, LANES), f32),
            pltpu.VMEM((2, rows, LANES), f32),
            pltpu.VMEM((4 * full_high, WIDE), f32),
            pltpu.VMEM((2, animals // WIDE, WIDE), f32),
            pltpu.VMEM((blocks, 2, markers), f32),
            pltpu.VMEM((layers, 2, gen), f32),
            pltpu.VMEM((blocks, 8, LANES), f32),
            dma((gen // chunk_rows,)),
            dma((blocks - 1,)),
            dma((blocks,)),
            dma((blocks - 1,)),
            dma((blocks,)),
            dma((blocks - 1,)),
            dma((blocks,)),
            dma((layers - 1,)),
            dma((layers,)),
            dma((blocks - 1,)),
            dma((blocks,)),
        ],
        compiler_params=pltpu.CompilerParams(
            collective_id=0, has_side_effects=True, vmem_limit_bytes=50 * 2**20
        ),
    )(
        hbm(direction),
        hbm(residual),
        hbm(record_inverse),
        hbm(precondition),
        hbm(genetic_inverse),
        hbm(sire_slot.reshape(rows, LANES)),
        hbm(dam_slot.reshape(rows, LANES)),
        hbm(sire_slot.reshape(1, animals)),
        hbm(dam_slot.reshape(1, animals)),
        hbm(send_rows.reshape(blocks, capacity)),
        hbm(genotyped_row.reshape(gen // LANES, LANES)),
        hbm(genotyped_row.reshape(1, gen)),
        hbm(allele_freq.reshape(1, markers)),
        hbm(marker_weight.reshape(1, markers)),
        hbm(genotypes),
        hbm(solution),
    )
    return pl.pallas_call(
        update,
        out_shape=(jax.ShapeDtypeStruct((2, animals), f32),) * 3,
        in_specs=[vmem] * 6,
        out_specs=(vmem,) * 3,
        compiler_params=pltpu.CompilerParams(vmem_limit_bytes=8 * 2**20),
    )(*[pltpu.with_memory_space_constraint(value, pltpu.VMEM) for value in carried])


def solution(mesh):
    return jax.shard_map(
        functools.partial(on_device, mesh.shape["anim"], mesh.shape["mark"]),
        mesh=mesh,
        in_specs=(
            P(None, "anim"),
            P(None, "anim"),
            P(None, "anim"),
            P(None, "anim"),
            P(None, "anim"),
            P(),
            P("anim"),
            P("anim"),
            P("anim", None, None),
            P("anim"),
            P("anim", "mark"),
            P("mark"),
            P("mark"),
        ),
        out_specs=(P(None, "anim"), P(None, "anim"), P(None, "anim")),
        check_vma=False,
    )
```
